128 devices in a mesh: samp: 16 (over z_lo, y, core), tp: 8 (over x, z_hi).
Axes of the slice: x: 4, y: 4, z: 4 (z_hi: 2, z_lo: 2; z = z_hi * 2 + z_lo), core: 2. Of those that a mesh axis runs over, the one named last changes fastest.
Arguments:
- prompt_rows: bfloat16 [32, 1536, 8, 2304], P('samp', None, 'tp'), may hold values from -6 to 6
- prompt_dt: bfloat16 [32, 1536, 8, 16], P('samp', None, 'tp'), may hold values from -3 to 3
- decode_rows: bfloat16 [32, 16, 2, 8, 2304], P(None, 'samp', None, 'tp'), may hold values from -6 to 6
- decode_dt: bfloat16 [32, 16, 2, 8, 16], P(None, 'samp', None, 'tp'), may hold values from -3 to 3
- placement: int32 [32], replicated, may hold values from 0 to 31, each once
- conv_weight: float32 [8, 4, 1280], P('tp'), may hold values from -3 to 3
- conv_bias: float32 [8, 1280], P('tp'), may hold values from -3 to 3
- dt_bias: float32 [8, 16], P('tp'), may hold values from -3 to -1.5
- a_log: float32 [8, 16], P('tp'), may hold values from -7.5 to -0.5
- skip_gain: float32 [8, 16], P('tp'), may hold values from -4 to 4
- norm_gain: float32 [8, 1024], P('tp'), may hold values from 0.1 to 1.9
Outputs:
- prefill_out: bfloat16 [32, 1536, 8, 1024], P('samp', 'tp')
- decode_out: bfloat16 [32, 16, 2, 8, 1024], P(None, 'samp', None, 'tp')
The draws below stay inside these ranges and needn't reach their ends.
Inputs may be any that keep to these rules, and one draw needn't show every extreme that they name: `placement`: every slot appears once.
All inputs are finite; a program needn't handle non-finite values.
Results may differ from the reference program's by a relative error of at most 0.001.
Values may be sent and summed in bfloat16 or wider, within the bound.
A program may use at most 192 MiB of HBM per device.

```python
import jax
import jax.numpy as jnp
from jax import lax

HG = 16
P_SIZE = 64
GROUPS = 8
CONV = 4
SPAN = 256
DSTEPS = 2
LEN = 1536
XBC = 1280
ROW = 2304
PROMPTS = 32
GROUP_SIZE = 16


def draw_a_log(key, part):
    key = jax.random.fold_in(key, 11)
    return jax.random.uniform(key, (GROUPS, HG), jnp.float32, -5.5, -0.5)


def block_levels(stream_key, shape, cuts, smallest, high):
    gain, own = 1.0, jax.random.fold_in(stream_key, 6)
    for dim, parts in cuts:
        heights = jnp.exp(jax.random.uniform(jax.random.fold_in(own, dim), (parts,), jnp.float32, smallest / len(cuts), high / len(cuts)))
        gain = gain * jnp.repeat(heights, shape[dim] // parts).reshape([-1 if axis == dim else 1 for axis in range(len(shape))])
    return gain


def gaussian(key, shape, deviation, limit, split=(), dtype=jnp.bfloat16):
    factor_of = block_levels(key, shape, split, -0.22, 0.18) if split else 1.0
    array = jax.random.normal(key, shape, jnp.float32) * deviation * factor_of
    return jnp.minimum(jnp.maximum(array, -limit), limit).astype(dtype)


def setup_inputs(seed: int = 0) -> dict:
    seeds = jax.random.split(jax.random.key(seed), 12)
    prompt_rows = gaussian(seeds[0], (PROMPTS, LEN, GROUPS, ROW), 1.0, 6.0, ((0, 16), (2, 8)))
    prompt_dt = gaussian(seeds[1], (PROMPTS, LEN, GROUPS, HG), 0.5, 3.0, ((0, 16), (2, 8)))
    decode_rows = gaussian(seeds[2], (PROMPTS, GROUP_SIZE, DSTEPS, GROUPS, ROW), 1.0, 6.0, ((1, 16), (3, 8)))
    decode_dt = gaussian(seeds[3], (PROMPTS, GROUP_SIZE, DSTEPS, GROUPS, HG), 0.5, 3.0, ((1, 16), (3, 8)))
    placement = jax.random.permutation(seeds[4], PROMPTS).astype(jnp.int32)
    conv_weight = gaussian(seeds[5], (GROUPS, CONV, XBC), 0.5, 3.0, ((0, 8),), jnp.float32)
    conv_bias = gaussian(seeds[6], (GROUPS, XBC), 0.5, 3.0, ((0, 8),), jnp.float32)
    dt_bias = jnp.clip(-3.0 + 1.5 * jax.random.uniform(seeds[7], (GROUPS, HG), jnp.float32) ** block_levels(seeds[7], (GROUPS, HG), ((0, 8),), -0.2, 0.2), -3.0, -1.5)
    a_log = draw_a_log(jax.random.fold_in(seeds[11], 71), 0)
    skip_gain = gaussian(seeds[9], (GROUPS, HG), 1.0, 4.0, ((0, 8),), jnp.float32)
    norm_gain = jnp.clip(1.0 + 0.18 * jax.random.normal(seeds[10], (GROUPS, HG * P_SIZE), jnp.float32), 0.1, 1.9)
    return dict(prompt_rows=prompt_rows, prompt_dt=prompt_dt, decode_rows=decode_rows, decode_dt=decode_dt, placement=placement, conv_weight=conv_weight, conv_bias=conv_bias, dt_bias=dt_bias, a_log=a_log, skip_gain=skip_gain, norm_gain=norm_gain)


highest = lax.Precision.HIGHEST
epsilon = 1e-05

def gated_norm(values, gate_in, norm_gain):
    gated = values * jax.nn.silu(gate_in)
    scale = lax.rsqrt(lax.optimization_barrier(jnp.mean(gated * gated, axis=-1, keepdims=True)) + epsilon)
    return (gated * scale * norm_gain).astype(jnp.bfloat16)

def prefill_group(token_rows, raw_dt, conv_weight, conv_bias, dt_bias, a_log, skip_gain, norm_gain):
    heads = raw_dt.shape[1]
    inner = norm_gain.shape[0]
    head_size = inner // heads
    channels = conv_bias.shape[0]
    state_size = (channels - inner) // 2
    length = token_rows.shape[0]
    taps = conv_weight.shape[0]
    mixed_in = token_rows[:, :channels].astype(jnp.float32)
    gate_in = token_rows[:, channels:].astype(jnp.float32)
    padded = jnp.concatenate([jnp.zeros((taps - 1, channels), jnp.float32), mixed_in], axis=0)
    convolved = conv_bias + sum((conv_weight[offset] * padded[offset:offset + length] for offset in range(taps)))
    convolved = jax.nn.silu(convolved)
    blocks = length // SPAN
    inputs_x = convolved[:, :inner].reshape(blocks, SPAN, heads, head_size)
    inputs_b = convolved[:, inner:inner + state_size].reshape(blocks, SPAN, state_size)
    inputs_c = convolved[:, inner + state_size:].reshape(blocks, SPAN, state_size)
    step_dt = jax.nn.softplus(raw_dt.astype(jnp.float32) + dt_bias)
    decay = (step_dt * -jnp.exp(a_log)).reshape(blocks, SPAN, heads)
    step_dt = step_dt.reshape(blocks, SPAN, heads)
    causal = jnp.arange(SPAN)[:, None] >= jnp.arange(SPAN)[None, :]

    def advance(carry_state, block):
        block_x, block_b, block_c, block_decay, block_dt = block
        cumulative = jnp.cumsum(block_decay, axis=0).T
        differences = cumulative[:, :, None] - cumulative[:, None, :]
        weights = jnp.exp(jnp.where(causal[None], differences, -jnp.inf))
        scores = jnp.dot(block_c, block_b.T, precision=highest, preferred_element_type=jnp.float32)
        weighted = weights * scores[None] * block_dt.T[:, None, :]
        within = jnp.einsum('hij,jhp->ihp', weighted, block_x, precision=highest)
        carried = jnp.einsum('in,hpn->ihp', block_c, carry_state, precision=highest) * jnp.exp(cumulative.T)[:, :, None]
        outputs = within + carried + skip_gain[None, :, None] * block_x
        final = cumulative[:, -1]
        leftover = jnp.exp(final[None, :] - cumulative.T) * block_dt
        new_state = jnp.exp(final)[:, None, None] * carry_state + jnp.einsum('jhp,jn->hpn', block_x * leftover[:, :, None], block_b, precision=highest)
        return (new_state, outputs)
    start_state = jnp.zeros((heads, head_size, state_size), jnp.float32)
    final_state, outputs = lax.scan(advance, start_state, (inputs_x, inputs_b, inputs_c, decay, step_dt))
    result = gated_norm(outputs.reshape(length, inner), gate_in, norm_gain)
    return (result, final_state, mixed_in[length - (taps - 1):])

def decode_group(carry_state, tail_rows, token_rows, raw_dt, conv_weight, conv_bias, dt_bias, a_log, skip_gain, norm_gain):
    heads = raw_dt.shape[1]
    inner = norm_gain.shape[0]
    head_size = inner // heads
    channels = conv_bias.shape[0]
    state_size = (channels - inner) // 2
    taps = conv_weight.shape[0]
    window = jnp.concatenate([tail_rows, token_rows[:, :channels].astype(jnp.float32)], axis=0)
    rate = -jnp.exp(a_log)
    results = []
    for position in range(token_rows.shape[0]):
        convolved = jax.nn.silu(conv_bias + sum((conv_weight[offset] * window[position + offset] for offset in range(taps))))
        current_x = convolved[:inner].reshape(heads, head_size)
        current_b = convolved[inner:inner + state_size]
        current_c = convolved[inner + state_size:]
        step_dt = jax.nn.softplus(raw_dt[position].astype(jnp.float32) + dt_bias)
        carry_state = jnp.exp(step_dt * rate)[:, None, None] * carry_state + (step_dt[:, None] * current_x)[:, :, None] * current_b[None, None, :]
        outputs = jnp.einsum('hpn,n->hp', carry_state, current_c, precision=highest) + skip_gain[:, None] * current_x
        results.append(gated_norm(outputs.reshape(inner), token_rows[position, channels:].astype(jnp.float32), norm_gain))
    return jnp.stack(results)

def group_prefill(token_rows, raw_dt, conv_weight, conv_bias, dt_bias, a_log, skip_gain, norm_gain):
    mapped = jax.vmap(prefill_group, in_axes=(1, 1, 0, 0, 0, 0, 0, 0), out_axes=(1, 0, 0))
    return mapped(token_rows, raw_dt, conv_weight, conv_bias, dt_bias, a_log, skip_gain, norm_gain)

def group_decode(states, tails, token_rows, raw_dt, conv_weight, conv_bias, dt_bias, a_log, skip_gain, norm_gain):
    over_groups = jax.vmap(decode_group, in_axes=(0, 0, 1, 1, 0, 0, 0, 0, 0, 0), out_axes=1)
    over_samples = jax.vmap(over_groups, in_axes=(None, None, 0, 0, None, None, None, None, None, None), out_axes=0)
    return over_samples(states, tails, token_rows, raw_dt, conv_weight, conv_bias, dt_bias, a_log, skip_gain, norm_gain)

def reference(prompt_rows, prompt_dt, decode_rows, decode_dt, placement, conv_weight, conv_bias, dt_bias, a_log, skip_gain, norm_gain):

    def one_prompt(pieces):
        return group_prefill(pieces[0], pieces[1], conv_weight, conv_bias, dt_bias, a_log, skip_gain, norm_gain)
    prefill_out, states, tails = lax.map(one_prompt, (prompt_rows, prompt_dt))
    chosen_states = states[placement]
    chosen_tails = tails[placement]

    def one_decode(pieces):
        return group_decode(pieces[0], pieces[1], pieces[2], pieces[3], conv_weight, conv_bias, dt_bias, a_log, skip_gain, norm_gain)
    decode_out = lax.map(one_decode, (chosen_states, chosen_tails, decode_rows, decode_dt))
    return (prefill_out, decode_out)
```

```python
import functools

import jax
import jax.numpy as jnp
from jax import lax
from jax.experimental import pallas as pl
from jax.experimental.pallas import tpu as pltpu
from jax.sharding import PartitionSpec as P

MESH = pl.DeviceIdType.MESH
HIGHEST = lax.Precision.HIGHEST
F32 = jnp.float32
BF16 = jnp.bfloat16
EPS = 1e-05

HEADS = 16
HEAD = 64
INNER = HEADS * HEAD
STATE = 128
XBC = INNER + 2 * STATE
ROW = XBC + INNER
SPAN = 128
HALF = SPAN // 2
TP = 8


def split(value):
    high = value.astype(BF16)
    return high, (value - high.astype(F32)).astype(BF16)


def silu_of_half(half):
    return half + half * jnp.tanh(half)


def softplus(value):
    return jnp.maximum(value, 0.0) + jnp.log1p(jnp.exp(-jnp.abs(value)))


def dot(left, right, precision=None):
    return jnp.dot(left, right, preferred_element_type=F32, precision=precision)


def dot_first(left, right):
    return lax.dot_general(left, right, (((0,), (0,)), ((), ())), preferred_element_type=F32)


def dot_last(left, right, precision=None):
    return lax.dot_general(
        left, right, (((1,), (1,)), ((), ())), preferred_element_type=F32, precision=precision
    )


def iota(shape, axis):
    return lax.broadcasted_iota(jnp.int32, shape, axis)


def kernel(
    ns,
    length,
    rows_hbm,
    raw_dt,
    drows,
    ddt,
    placement,
    conv_w,
    conv_b,
    dt_bias,
    a_log,
    skip_gain,
    norm_gain,
    gathered,
    dec_out,
    rows,
    outs,
    xs,
    mats,
    bcs,
    fac_in,
    fac_out,
    ends,
    expand,
    fx,
    gated,
    state,
    finals,
    halfw,
    skip,
    perm,
    perm2,
    dpieces,
    dsend,
    drecv,
    dtable,
    osend,
    orecv,
    in_sem,
    send_sem,
    recv_sem,
    own_sem,
    dsend_sem,
    drecv_sem,
    osend_sem,
    orecv_sem,
):
    me = lax.axis_index("tp")
    sm = lax.axis_index("samp")
    x0 = me // 2
    chunks = length // SPAN
    n256 = 16 * ns

    def rows_in(p, c):
        part = pl.ds(pl.multiple_of(c * SPAN, SPAN), SPAN)
        return pltpu.make_async_copy(rows_hbm.at[p, part], rows.at[p, part], in_sem.at[p, c])

    for p in range(2):
        lax.fori_loop(0, chunks, lambda c, _: (rows_in(p, c).start(), 0)[1], 0)

    barrier = pltpu.get_barrier_semaphore()
    for d in range(1, TP):
        pl.semaphore_signal(
            barrier, inc=1, device_id={"tp": lax.rem(me + d, TP)}, device_id_type=MESH
        )
    for d in range(1, ns):
        pl.semaphore_signal(
            barrier, inc=1, device_id={"samp": lax.rem(sm + d, ns)}, device_id_type=MESH
        )

    halfw[0:4, :] = conv_w[...] * 0.5
    halfw[4:5, :] = conv_b[...] * 0.5
    eye = iota((HEADS, HEADS), 0) == iota((HEADS, HEADS), 1)

    def column(row):
        return jnp.sum(jnp.where(eye, row, 0.0), axis=1, keepdims=True)

    bias_row = dt_bias[...]
    rate_row = -jnp.exp(a_log[...])
    bias_col = column(bias_row)
    rate_col = column(rate_row)
    own = (iota((HEADS, INNER), 0) == iota((HEADS, INNER), 1) // HEAD).astype(F32)
    expand[0:HEADS, :] = own.astype(BF16)
    expand[HEADS : 2 * HEADS, :] = own.astype(BF16)
    skip[...] = jnp.sum(own * column(skip_gain[...]), axis=0, keepdims=True)

    upper = (iota((SPAN, SPAN), 0) <= iota((SPAN, SPAN), 1)).astype(F32)
    for p in range(2):
        step = softplus(raw_dt[p].astype(F32) + bias_col)
        steps = jnp.concatenate([step[:, c * SPAN : (c + 1) * SPAN] for c in range(chunks)], axis=0)
        decay = steps * jnp.concatenate([rate_col] * chunks, axis=0)
        total = dot(decay, upper, HIGHEST)
        middle = 0.5 * total[:, SPAN - 1 : SPAN]
        from_middle = total - middle
        in_high, in_low = split(jnp.exp(-from_middle) * steps)
        out_high, out_low = split(jnp.exp(from_middle))
        for c in range(chunks):
            part = slice(c * HEADS, (c + 1) * HEADS)
            fac_in[p * chunks + c, 0:HEADS, :] = in_high[part]
            fac_in[p * chunks + c, HEADS : 2 * HEADS, :] = in_low[part]
            fac_out[p * chunks + c, 0:HEADS, :] = out_high[part]
            fac_out[p * chunks + c, HEADS : 2 * HEADS, :] = out_low[part]
            ends[p * chunks + c] = jnp.broadcast_to(
                jnp.sum(own * jnp.exp(middle[part]), axis=0, keepdims=True), (8, INNER)
            )

    lanes = iota((1, n256), 1)
    slot_of = jnp.zeros((1, n256), jnp.int32)
    for prompt in range(2 * ns):
        slot_of = jnp.where((lanes // 2) % (2 * ns) == prompt, placement[prompt], slot_of)
    r = iota((n256, n256), 0)
    s = iota((n256, n256), 1)
    q_of_s = s // (4 * ns)
    perm[...] = jnp.where(
        ((r // 4) % 4 == q_of_s) & (slot_of == 2 * (r // 16) + (r // 2) % 2) & (r % 2 == s % 2),
        1.0,
        0.0,
    ).astype(BF16)
    perm2[...] = jnp.where(
        (r // (4 * ns) == (s // 4) % 4) & ((r // ns) % 4 == s % 4) & (r % ns == s // 16), 1.0, 0.0
    ).astype(BF16)
    n64 = 4 * ns
    dstep = jnp.zeros((n64, HEADS), F32)
    for i in range(2):
        pick = jnp.where(
            iota((n64, 2 * ns), 0) == 2 * iota((n64, 2 * ns), 1) + i, 1.0, 0.0
        ).astype(BF16)
        dstep = dstep + dot_last(pick, ddt[i])
    dpieces[...] = jnp.zeros_like(dpieces)
    for q in range(4):
        dpieces[q * n64 : (q + 1) * n64, 0:512] = drows[:, q * 512 : (q + 1) * 512]
    for q in range(2):
        dpieces[q * n64 : (q + 1) * n64, 512:640] = drows[:, 2048 + q * 128 : 2176 + q * 128]
    dpieces[2 * n64 : 3 * n64, 512 : 512 + HEADS] = dstep.astype(BF16)
    dsend[...] = dot(perm[...], dpieces[...]).astype(BF16)

    pl.semaphore_wait(barrier, TP - 1 + ns - 1)

    def block_of(k):
        return pl.ds(pl.multiple_of(16 * k, 16), 16)

    def to_holder(d):
        peer = lax.rem(sm + d, ns)
        return pltpu.make_async_remote_copy(
            src_ref=dsend.at[block_of(peer)],
            dst_ref=drecv.at[block_of(sm)],
            send_sem=dsend_sem,
            recv_sem=drecv_sem,
            device_id={"samp": peer},
            device_id_type=MESH,
        )

    for d in range(1, ns):
        to_holder(d).start()
    drecv[block_of(sm), :] = dsend[block_of(sm), :]

    def conv_half(p, c, columns):
        base = pl.multiple_of(c * SPAN, SPAN)
        before = pl.multiple_of(jnp.maximum(base - 16, 0), 16)
        keep = jnp.where(c > 0, 1.0, 0.0).astype(F32)
        now = rows[p, pl.ds(base, SPAN), columns].astype(F32)
        last = rows[p, pl.ds(before, 16), columns].astype(F32)[8:16] * keep
        both = jnp.concatenate([last, now], axis=0)
        result = halfw[4:5, columns] + halfw[3:4, columns] * now
        for back in range(1, 4):
            result = result + halfw[3 - back : 4 - back, columns] * pltpu.roll(both, back, 0)[8:]
        return result

    def first_pass(p):
        state[...] = jnp.zeros_like(state)

        def body(c, _):
            index = p * chunks + c
            rows_in(p, c).wait()
            part = pl.ds(pl.multiple_of(c * SPAN, SPAN), SPAN)
            fx[...] = dot_first(fac_in[index], expand[...])
            for b in range(INNER // 128):
                columns = slice(b * 128, (b + 1) * 128)
                x = silu_of_half(conv_half(p, c, columns))
                xs[part, columns] = x
                high, low = split(x * fx[:, columns])
                mats[c, 0:128, columns] = low
                mats[c, 128:256, columns] = high
            for b in range(2):
                columns = slice(INNER + b * 128, INNER + (b + 1) * 128)
                bcs[c, :, b * 128 : (b + 1) * 128] = silu_of_half(conv_half(p, c, columns))
            b_high, b_low = split(bcs[c, :, 0:128].T)
            b_twice = jnp.concatenate([b_high, b_high], axis=1)
            for b in range(INNER // 256):
                columns = slice(b * 256, (b + 1) * 256)
                end = ends[index, 0:1, columns]
                entering = state[:, columns] * end
                high, low = split(entering)
                mats[c, 256:384, columns] = high
                mats[c, 384:512, columns] = low
                added = dot(b_twice, mats[c, 0:256, columns]) + dot(b_low, mats[c, 128:256, columns])
                state[:, columns] = end * (added + entering)
            return 0

        lax.fori_loop(0, chunks, body, 0)
        finals[p] = state[...]

    def second_pass(p):
        def body(k, _):
            unit = lax.rem(x0 + 1 + lax.rem(k, 4), 4)
            third = jnp.where(lax.rem(k, 2) == 0, k // 4, 2 - k // 4)
            c = 3 * unit + third
            index = p * chunks + c
            base = pl.multiple_of(c * SPAN, SPAN)
            part = pl.ds(base, SPAN)
            fx[...] = dot_first(fac_out[index], expand[...])
            b_now = bcs[c, :, 0:128]
            c_now = bcs[c, :, 128:256]
            scores = dot_last(c_now, b_now, HIGHEST)
            scores = jnp.where(iota((SPAN, SPAN), 0) >= iota((SPAN, SPAN), 1), scores, 0.0)
            s_high, s_low = split(scores)
            c_high, c_low = split(c_now)
            left = jnp.concatenate([s_high, s_high, c_high, c_high], axis=1)
            left_low = jnp.concatenate([s_low, c_low], axis=1)
            squares = jnp.zeros((SPAN, 128), F32)
            for b in range(INNER // 256):
                columns = slice(b * 256, (b + 1) * 256)
                y = dot(left, mats[c, :, columns]) + dot(left_low, mats[c, 128:384, columns])
                y = fx[:, columns] * y + skip[:, columns] * xs[part, columns]
                z_half = 0.5 * rows[p, part, XBC + b * 256 : XBC + (b + 1) * 256].astype(F32)
                g = y * silu_of_half(z_half)
                gated[:, columns] = g
                squares = squares + g[:, 0:128] * g[:, 0:128] + g[:, 128:256] * g[:, 128:256]
            mean = jnp.sum(squares, axis=1, keepdims=True) * (1.0 / INNER)
            scale = lax.rsqrt(mean + EPS)
            for b in range(INNER // 128):
                columns = slice(b * 128, (b + 1) * 128)
                outs[p, part, columns] = (gated[:, columns] * scale * norm_gain[:, columns]).astype(
                    BF16
                )
            for half in range(2):
                piece = 2 * third + half
                dest = 2 * unit + piece // 3
                source = outs.at[p, pl.ds(pl.multiple_of(base + half * HALF, HALF), HALF)]
                place = pl.ds(pl.multiple_of(lax.rem(piece, 3) * HALF, HALF), HALF)
                target = gathered.at[me, p, place]

                @pl.when(dest != me)
                def _():
                    pltpu.make_async_remote_copy(
                        src_ref=source,
                        dst_ref=target,
                        send_sem=send_sem.at[dest],
                        recv_sem=recv_sem.at[me],
                        device_id={"tp": dest},
                        device_id_type=MESH,
                    ).start()

                @pl.when(dest == me)
                def _():
                    pltpu.make_async_copy(source, target, own_sem).start()

            return 0

        lax.fori_loop(0, chunks, body, 0)

    first_pass(0)
    second_pass(0)
    first_pass(1)

    for d in range(1, ns):
        to_holder(d).wait_send()
    pltpu.make_async_copy(
        drecv.at[pl.ds(0, 16 * (ns - 1))], drecv.at[pl.ds(0, 16 * (ns - 1))], drecv_sem
    ).wait()
    dtable[...] = dot(perm2[...], drecv[...])
    pieces = []
    for j in range(2):
        tail = rows[j, length - 16 : length, 0:XBC].astype(F32)
        window = [tail[13:14], tail[14:15], tail[15:16]]
        gates, steps = [], []
        for i in range(2):
            at = [slice(q * n64 + (2 * j + i) * ns, q * n64 + (2 * j + i + 1) * ns) for q in range(4)]
            window.append(
                jnp.concatenate(
                    [dtable[at[0], 0:512], dtable[at[1], 0:512], dtable[at[2], 0:256]], axis=1
                )
            )
            gates.append(
                jnp.concatenate(
                    [
                        dtable[at[2], 256:512],
                        dtable[at[3], 0:512],
                        dtable[at[0], 512:640],
                        dtable[at[1], 512:640],
                    ],
                    axis=1,
                )
            )
            steps.append(softplus(dtable[at[2], 512 : 512 + HEADS] + bias_row))
        convs = []
        for i in range(2):
            half = halfw[4:5, :]
            for tap in range(4):
                half = half + halfw[tap : tap + 1, :] * window[i + tap]
            convs.append(silu_of_half(half))
        x = [v[:, 0:INNER] for v in convs]
        b = [v[:, INNER : INNER + STATE] for v in convs]
        cc = [v[:, INNER + STATE : XBC] for v in convs]
        from_state = dot(jnp.concatenate(cc, axis=0), finals[j], HIGHEST)
        wide_dt = [dot(v, own, HIGHEST) for v in steps]
        wide_decay = [dot(jnp.exp(v * rate_row), own, HIGHEST) for v in steps]

        def over(i, k):
            return jnp.sum(b[i] * cc[k], axis=1, keepdims=True)

        first = wide_dt[0] * x[0]
        second = wide_dt[1] * x[1]
        y = [
            wide_decay[0] * from_state[0:ns] + first * over(0, 0) + skip[...] * x[0],
            wide_decay[1] * (wide_decay[0] * from_state[ns : 2 * ns] + first * over(0, 1))
            + second * over(1, 1)
            + skip[...] * x[1],
        ]
        for i in range(2):
            g = y[i] * silu_of_half(0.5 * gates[i])
            scale = lax.rsqrt(jnp.sum(g * g, axis=1, keepdims=True) * (1.0 / INNER) + EPS)
            pieces.append((g * scale * norm_gain[...]).astype(BF16))
    table = jnp.concatenate(
        [v[:, q * 256 : (q + 1) * 256] for q in range(4) for v in pieces], axis=0
    )
    osend[...] = dot_first(perm2[...], table).astype(BF16)

    def to_sample(d):
        peer = lax.rem(sm + d, ns)
        return pltpu.make_async_remote_copy(
            src_ref=osend.at[block_of(peer)],
            dst_ref=orecv.at[block_of(sm)],
            send_sem=osend_sem,
            recv_sem=orecv_sem,
            device_id={"samp": peer},
            device_id_type=MESH,
        )

    for d in range(1, ns):
        to_sample(d).start()
    orecv[block_of(sm), :] = osend[block_of(sm), :]

    second_pass(1)

    pltpu.make_async_copy(
        osend.at[pl.ds(0, 16 * (ns - 1))], osend.at[pl.ds(0, 16 * (ns - 1))], osend_sem
    ).wait()
    pltpu.make_async_copy(
        orecv.at[pl.ds(0, 16 * (ns - 1))], orecv.at[pl.ds(0, 16 * (ns - 1))], orecv_sem
    ).wait()
    table = dot_first(perm[...], orecv[...]).astype(BF16)
    for q in range(4):
        dec_out[:, q * 256 : (q + 1) * 256] = table[q * n64 : (q + 1) * n64]

    pltpu.make_async_copy(gathered.at[me], gathered.at[me], own_sem).wait()
    for d in range(1, TP):
        peer = lax.rem(me + d, TP)
        pltpu.make_async_copy(gathered.at[peer], gathered.at[peer], send_sem.at[peer]).wait()
        pltpu.make_async_copy(gathered.at[peer], gathered.at[peer], recv_sem.at[peer]).wait()


def per_device(
    ns,
    prompt_rows,
    prompt_dt,
    decode_rows,
    decode_dt,
    placement,
    conv_weight,
    conv_bias,
    dt_bias,
    a_log,
    skip_gain,
    norm_gain,
):
    length = prompt_rows.shape[1]
    chunks = length // SPAN
    n64, n256 = 4 * ns, 16 * ns
    vmem = pl.BlockSpec(memory_space=pltpu.VMEM)
    hbm = pl.BlockSpec(memory_space=pl.ANY)
    gathered, dec = pl.pallas_call(
        functools.partial(kernel, ns, length),
        out_shape=(
            jax.ShapeDtypeStruct((TP, 2, length // TP, INNER), BF16),
            jax.ShapeDtypeStruct((n64, INNER), BF16),
        ),
        in_specs=[hbm, vmem, vmem, vmem, pl.BlockSpec(memory_space=pltpu.SMEM)] + [vmem] * 6,
        out_specs=(hbm, vmem),
        scratch_shapes=[
            pltpu.VMEM((2, length, ROW), BF16),
            pltpu.VMEM((2, length, INNER), BF16),
            pltpu.VMEM((length, INNER), F32),
            pltpu.VMEM((chunks, 4 * SPAN, INNER), BF16),
            pltpu.VMEM((chunks, SPAN, 2 * STATE), F32),
            pltpu.VMEM((2 * chunks, 2 * HEADS, SPAN), BF16),
            pltpu.VMEM((2 * chunks, 2 * HEADS, SPAN), BF16),
            pltpu.VMEM((2 * chunks, 8, INNER), F32),
            pltpu.VMEM((2 * HEADS, INNER), BF16),
            pltpu.VMEM((SPAN, INNER), F32),
            pltpu.VMEM((SPAN, INNER), F32),
            pltpu.VMEM((STATE, INNER), F32),
            pltpu.VMEM((2, STATE, INNER), F32),
            pltpu.VMEM((8, XBC), F32),
            pltpu.VMEM((1, INNER), F32),
            pltpu.VMEM((n256, n256), BF16),
            pltpu.VMEM((n256, n256), BF16),
            pltpu.VMEM((n256, 640), BF16),
            pltpu.VMEM((n256, 640), BF16),
            pltpu.VMEM((n256, 640), BF16),
            pltpu.VMEM((n256, 640), F32),
            pltpu.VMEM((n256, 256), BF16),
            pltpu.VMEM((n256, 256), BF16),
            pltpu.SemaphoreType.DMA((2, chunks)),
            pltpu.SemaphoreType.DMA((TP,)),
            pltpu.SemaphoreType.DMA((TP,)),
            pltpu.SemaphoreType.DMA,
            pltpu.SemaphoreType.DMA,
            pltpu.SemaphoreType.DMA,
            pltpu.SemaphoreType.DMA,
            pltpu.SemaphoreType.DMA,
        ],
        compiler_params=pltpu.CompilerParams(
            collective_id=0, has_side_effects=True, vmem_limit_bytes=58 * 2**20
        ),
    )(
        prompt_rows[:, :, 0, :],
        prompt_dt[:, :, 0, :].transpose(0, 2, 1),
        decode_rows.reshape(n64, ROW),
        decode_dt[:, 0, :, 0, :].transpose(1, 2, 0),
        placement,
        conv_weight[0],
        conv_bias,
        dt_bias,
        a_log,
        skip_gain,
        norm_gain,
    )
    prefill_out = gathered.transpose(1, 2, 0, 3)
    return prefill_out, dec.reshape(2 * ns, 1, 2, 1, INNER)


def solution(mesh):
    in_specs = (
        P("samp", None, "tp", None),
        P("samp", None, "tp", None),
        P(None, "samp", None, "tp", None),
        P(None, "samp", None, "tp", None),
        P(),
        P("tp", None, None),
        P("tp", None),
        P("tp", None),
        P("tp", None),
        P("tp", None),
        P("tp", None),
    )
    out_specs = (P("samp", "tp", None, None), P(None, "samp", None, "tp", None))
    return jax.shard_map(
        functools.partial(per_device, mesh.shape["samp"]),
        mesh=mesh,
        in_specs=in_specs,
        out_specs=out_specs,
        check_vma=False,
    )
```

```python
import functools

import jax
import jax.numpy as jnp
from jax import lax
from jax.experimental import pallas as pl
from jax.experimental.pallas import tpu as pltpu
from jax.sharding import PartitionSpec as P

MESH = pl.DeviceIdType.MESH
HIGHEST = lax.Precision.HIGHEST
F32 = jnp.float32
BF16 = jnp.bfloat16
EPS = 1e-05

HEADS = 16
HEAD = 64
INNER = HEADS * HEAD
STATE = 128
XBC = INNER + 2 * STATE
ROW = XBC + INNER
SPAN = 128
HALF = SPAN // 2
TP = 8


def split(value):
    high = value.astype(BF16)
    return high, (value - high.astype(F32)).astype(BF16)


def silu_of_half(half):
    return half + half * jnp.tanh(half)


def softplus(value):
    return jnp.maximum(value, 0.0) + jnp.log1p(jnp.exp(-jnp.abs(value)))


def dot(left, right, precision=None):
    return jnp.dot(left, right, preferred_element_type=F32, precision=precision)


def dot_first(left, right):
    return lax.dot_general(left, right, (((0,), (0,)), ((), ())), preferred_element_type=F32)


def dot_last(left, right, precision=None):
    return lax.dot_general(
        left, right, (((1,), (1,)), ((), ())), preferred_element_type=F32, precision=precision
    )


def iota(shape, axis):
    return lax.broadcasted_iota(jnp.int32, shape, axis)


def kernel(
    ns,
    length,
    rows_hbm,
    raw_dt,
    drows,
    ddt,
    placement,
    conv_w,
    conv_b,
    dt_bias,
    a_log,
    skip_gain,
    norm_gain,
    final,
    dec_out,
    gathered,
    rows,
    carry,
    xs,
    mats,
    bcs,
    fac_in,
    fac_out,
    ends,
    expand,
    fx,
    gated,
    state,
    halfw,
    skip,
    perm,
    perm2,
    perm3,
    dpieces,
    dsend,
    drecv,
    dtable,
    osend,
    orecv,
    in_sem,
    send_sem,
    recv_sem,
    own_sem,
    dsend_sem,
    drecv_sem,
    osend_sem,
    orecv_sem,
):
    me = lax.axis_index("tp")
    sm = lax.axis_index("samp")
    x0 = me // 2
    chunks = length // SPAN
    n256 = 16 * ns

    def rows_in(p, c):
        part = pl.ds(pl.multiple_of(c * SPAN, SPAN), SPAN)
        return pltpu.make_async_copy(rows_hbm.at[p, part], rows.at[p, part], in_sem.at[p, c])

    lax.fori_loop(0, chunks, lambda c, _: (rows_in(0, c).start(), 0)[1], 0)

    barrier = pltpu.get_barrier_semaphore()
    for d in range(1, TP):
        pl.semaphore_signal(
            barrier, inc=1, device_id={"tp": lax.rem(me + d, TP)}, device_id_type=MESH
        )
    for d in range(1, ns):
        pl.semaphore_signal(
            barrier, inc=1, device_id={"samp": lax.rem(sm + d, ns)}, device_id_type=MESH
        )

    halfw[0:4, :] = conv_w[...] * 0.5
    halfw[4:5, :] = conv_b[...] * 0.5
    eye = iota((HEADS, HEADS), 0) == iota((HEADS, HEADS), 1)

    def column(row):
        return jnp.sum(jnp.where(eye, row, 0.0), axis=1, keepdims=True)

    bias_row = dt_bias[...]
    rate_row = -jnp.exp(a_log[...])
    bias_col = column(bias_row)
    rate_col = column(rate_row)
    own = (iota((HEADS, INNER), 0) == iota((HEADS, INNER), 1) // HEAD).astype(F32)
    expand[0:HEADS, :] = own.astype(BF16)
    expand[HEADS : 2 * HEADS, :] = own.astype(BF16)
    skip[...] = jnp.sum(own * column(skip_gain[...]), axis=0, keepdims=True)

    def prepare(p):
        upper = (iota((SPAN, SPAN), 0) <= iota((SPAN, SPAN), 1)).astype(F32)
        step = softplus(raw_dt[p].astype(F32) + bias_col)
        steps = jnp.concatenate([step[:, c * SPAN : (c + 1) * SPAN] for c in range(chunks)], axis=0)
        decay = steps * jnp.concatenate([rate_col] * chunks, axis=0)
        total = dot(decay, upper, HIGHEST)
        middle = 0.5 * total[:, SPAN - 1 : SPAN]
        from_middle = total - middle
        in_high, in_low = split(jnp.exp(-from_middle) * steps)
        out_high, out_low = split(jnp.exp(from_middle))
        for c in range(chunks):
            part = slice(c * HEADS, (c + 1) * HEADS)
            fac_in[c, 0:HEADS, :] = in_high[part]
            fac_in[c, HEADS : 2 * HEADS, :] = in_low[part]
            fac_out[c, 0:HEADS, :] = out_high[part]
            fac_out[c, HEADS : 2 * HEADS, :] = out_low[part]
            ends[c] = jnp.broadcast_to(
                jnp.sum(own * jnp.exp(middle[part]), axis=0, keepdims=True), (8, INNER)
            )

    n64 = 4 * ns
    n32 = 2 * ns

    def block_of(k):
        return pl.ds(pl.multiple_of(16 * k, 16), 16)

    def to_holder(d):
        peer = lax.rem(sm + d, ns)
        return pltpu.make_async_remote_copy(
            src_ref=dsend.at[block_of(peer)],
            dst_ref=drecv.at[block_of(sm)],
            send_sem=dsend_sem,
            recv_sem=drecv_sem,
            device_id={"samp": peer},
            device_id_type=MESH,
        )

    def sort_decode_rows():
        lanes = iota((1, n256), 1)
        slot_of = jnp.zeros((1, n256), jnp.int32)
        for prompt in range(n32):
            slot_of = jnp.where(lanes % n32 == prompt, placement[prompt], slot_of)
        r = iota((n256, n256), 0)
        s = iota((n256, n256), 1)
        perm[...] = jnp.where(
            ((r // 4) % 4 == s // n64)
            & (slot_of == 2 * (r // 16) + (r // 2) % 2)
            & (r % 2 == (s // n32) % 2),
            1.0,
            0.0,
        ).astype(BF16)
        perm2[...] = jnp.where(
            (r // n64 == (s // 4) % 4) & ((r // ns) % 4 == s % 4) & (r % ns == s // 16), 1.0, 0.0
        ).astype(BF16)
        r = iota((256, 256), 0)
        s = iota((256, 256), 1)
        perm3[...] = jnp.where((r % TP == s // 32) & (r // TP == s % 32), 1.0, 0.0).astype(BF16)
        unit = jnp.where(iota((n32, n32), 0) == iota((n32, n32), 1), 1.0, 0.0).astype(BF16)
        dpieces[...] = jnp.zeros_like(dpieces)
        for i in range(2):
            for q in range(4):
                part = slice(q * n64 + i * n32, q * n64 + (i + 1) * n32)
                dpieces[part, 0:512] = drows[i, :, q * 512 : (q + 1) * 512]
                if q < 2:
                    dpieces[part, 512:640] = drows[i, :, 2048 + q * 128 : 2176 + q * 128]
                if q == 2:
                    dpieces[part, 512 : 512 + HEADS] = dot_last(unit, ddt[i]).astype(BF16)
        dsend[...] = dot(perm[...], dpieces[...]).astype(BF16)
        drecv[block_of(sm), :] = dsend[block_of(sm), :]

    def conv_half(now, last, columns):
        both = jnp.concatenate([last, now], axis=0)
        result = halfw[4:5, columns] + halfw[3:4, columns] * now
        for back in range(1, 4):
            result = result + halfw[3 - back : 4 - back, columns] * pltpu.roll(both, back, 0)[8:]
        return result

    def first_pass(p, c):
        rows_in(p, c).wait()
        base = pl.multiple_of(c * SPAN, SPAN)
        part = pl.ds(base, SPAN)
        keep = jnp.where(c > 0, 1.0, 0.0).astype(F32)
        fx[...] = dot_first(fac_in[c], expand[...])
        for b in range(XBC // 128):
            columns = slice(b * 128, (b + 1) * 128)
            now = rows[p, part, columns].astype(F32)
            last = carry[p, :, columns].astype(F32)[8:16] * keep
            value = silu_of_half(conv_half(now, last, columns))
            if b < INNER // 128:
                xs[part, columns] = value
                high, low = split(value * fx[:, columns])
                mats[c, 0:128, columns] = low
                mats[c, 128:256, columns] = high
            else:
                bcs[c, :, b * 128 - INNER : (b + 1) * 128 - INNER] = value
        carry[p] = rows[p, pl.ds(pl.multiple_of(base + SPAN - 16, 16), 16), 0:XBC]
        b_high, b_low = split(bcs[c, :, 0:128].T)
        b_twice = jnp.concatenate([b_high, b_high], axis=1)
        for b in range(INNER // 256):
            columns = slice(b * 256, (b + 1) * 256)
            end = ends[c, 0:1, columns]
            entering = state[p, :, columns] * end
            high, low = split(entering)
            mats[c, 256:384, columns] = high
            mats[c, 384:512, columns] = low
            added = dot(b_twice, mats[c, 0:256, columns]) + dot(b_low, mats[c, 128:256, columns])
            state[p, :, columns] = end * (added + entering)

    def second_pass(p, unit, third):
        c = 3 * unit + third
        base = pl.multiple_of(c * SPAN, SPAN)
        part = pl.ds(base, SPAN)
        fx[...] = dot_first(fac_out[c], expand[...])
        b_now = bcs[c, :, 0:128]
        c_now = bcs[c, :, 128:256]
        scores = dot_last(c_now, b_now, HIGHEST)
        scores = jnp.where(iota((SPAN, SPAN), 0) >= iota((SPAN, SPAN), 1), scores, 0.0)
        s_high, s_low = split(scores)
        c_high, c_low = split(c_now)
        left = jnp.concatenate([s_high, s_high, c_high, c_high], axis=1)
        left_low = jnp.concatenate([s_low, c_low], axis=1)
        squares = jnp.zeros((SPAN, 128), F32)
        for b in range(INNER // 256):
            columns = slice(b * 256, (b + 1) * 256)
            y = dot(left, mats[c, :, columns]) + dot(left_low, mats[c, 128:384, columns])
            y = fx[:, columns] * y + skip[:, columns] * xs[part, columns]
            z_half = 0.5 * rows[p, part, XBC + b * 256 : XBC + (b + 1) * 256].astype(F32)
            g = y * silu_of_half(z_half)
            gated[:, columns] = g
            squares = squares + g[:, 0:128] * g[:, 0:128] + g[:, 128:256] * g[:, 128:256]
        mean = jnp.sum(squares, axis=1, keepdims=True) * (1.0 / INNER)
        scale = lax.rsqrt(mean + EPS)
        for b in range(INNER // 128):
            columns = slice(b * 128, (b + 1) * 128)
            rows[p, part, columns] = (gated[:, columns] * scale * norm_gain[:, columns]).astype(BF16)
        for half in range(2):
            piece = 2 * third + half
            dest = 2 * unit + piece // 3
            rank = lax.rem(piece, 3)
            source = rows.at[p, pl.ds(pl.multiple_of(base + half * HALF, HALF), HALF), pl.ds(0, INNER)]
            target = gathered.at[me, p, pl.ds(pl.multiple_of(rank * HALF, HALF), HALF)]

            @pl.when(dest != me)
            def _():
                pltpu.make_async_remote_copy(
                    src_ref=source,
                    dst_ref=target,
                    send_sem=send_sem.at[dest],
                    recv_sem=recv_sem.at[p, rank],
                    device_id={"tp": dest},
                    device_id_type=MESH,
                ).start()

            @pl.when(dest == me)
            def _():
                pltpu.make_async_copy(source, target, own_sem).start()

    def decode():
        for d in range(1, ns):
            to_holder(d).wait_send()
        pltpu.make_async_copy(
            drecv.at[pl.ds(0, 16 * (ns - 1))], drecv.at[pl.ds(0, 16 * (ns - 1))], drecv_sem
        ).wait()
        dtable[...] = dot(perm2[...], drecv[...])
        pieces = []
        for j in range(2):
            tail = carry[j].astype(F32)
            window = [tail[13:14], tail[14:15], tail[15:16]]
            gates, steps = [], []
            for i in range(2):
                at = [slice(q * n64 + (2 * j + i) * ns, q * n64 + (2 * j + i + 1) * ns) for q in range(4)]
                window.append(
                    jnp.concatenate(
                        [dtable[at[0], 0:512], dtable[at[1], 0:512], dtable[at[2], 0:256]], axis=1
                    )
                )
                gates.append(
                    jnp.concatenate(
                        [
                            dtable[at[2], 256:512],
                            dtable[at[3], 0:512],
                            dtable[at[0], 512:640],
                            dtable[at[1], 512:640],
                        ],
                        axis=1,
                    )
                )
                steps.append(softplus(dtable[at[2], 512 : 512 + HEADS] + bias_row))
            convs = []
            for i in range(2):
                half = halfw[4:5, :]
                for tap in range(4):
                    half = half + halfw[tap : tap + 1, :] * window[i + tap]
                convs.append(silu_of_half(half))
            x = [v[:, 0:INNER] for v in convs]
            b = [v[:, INNER : INNER + STATE] for v in convs]
            cc = [v[:, INNER + STATE : XBC] for v in convs]
            from_state = dot(jnp.concatenate(cc, axis=0), state[j], HIGHEST)
            wide_dt = [dot(v, own, HIGHEST) for v in steps]
            wide_decay = [dot(jnp.exp(v * rate_row), own, HIGHEST) for v in steps]

            def over(i, k):
                return jnp.sum(b[i] * cc[k], axis=1, keepdims=True)

            first = wide_dt[0] * x[0]
            second = wide_dt[1] * x[1]
            y = [
                wide_decay[0] * from_state[0:ns] + first * over(0, 0) + skip[...] * x[0],
                wide_decay[1] * (wide_decay[0] * from_state[ns : 2 * ns] + first * over(0, 1))
                + second * over(1, 1)
                + skip[...] * x[1],
            ]
            for i in range(2):
                g = y[i] * silu_of_half(0.5 * gates[i])
                scale = lax.rsqrt(jnp.sum(g * g, axis=1, keepdims=True) * (1.0 / INNER) + EPS)
                pieces.append((g * scale * norm_gain[...]).astype(BF16))
        table = jnp.concatenate(
            [v[:, q * 256 : (q + 1) * 256] for q in range(4) for v in pieces], axis=0
        )
        osend[...] = dot_first(perm2[...], table).astype(BF16)

        for d in range(1, ns):
            to_sample(d).start()
        orecv[block_of(sm), :] = osend[block_of(sm), :]

    def to_sample(d):
        peer = lax.rem(sm + d, ns)
        return pltpu.make_async_remote_copy(
            src_ref=osend.at[block_of(peer)],
            dst_ref=orecv.at[block_of(sm)],
            send_sem=osend_sem,
            recv_sem=orecv_sem,
            device_id={"samp": peer},
            device_id_type=MESH,
        )

    state[...] = jnp.zeros_like(state)
    carry[...] = jnp.zeros_like(carry)
    prepare(0)
    sort_decode_rows()
    lax.fori_loop(0, chunks, lambda c, _: (first_pass(0, c), 0)[1], 0)
    pl.semaphore_wait(barrier, TP - 1 + ns - 1)
    for d in range(1, ns):
        to_holder(d).start()

    def body(t, _):
        p = t // (2 * chunks)
        u = lax.rem(t, 2 * chunks)
        is_first = (p == 1) & (u < chunks)

        @pl.when(t == chunks + 3)
        def _():
            lax.fori_loop(0, chunks, lambda c, _: (rows_in(1, c).start(), 0)[1], 0)

        @pl.when(t == 2 * chunks)
        def _():
            prepare(1)

        @pl.when(is_first)
        def _():
            first_pass(p, u)

        @pl.when(jnp.logical_not(is_first))
        def _():
            k = u - chunks
            lane = lax.rem(k, 4)
            unit = lax.rem(x0 + 1 + lane, 4)
            row = k // 4
            second_pass(p, unit, jnp.where(lax.rem(lane, 2) == 0, row, 2 - row))

        @pl.when(t == 3 * chunks - 1)
        def _():
            decode()

        return 0

    lax.fori_loop(chunks, 4 * chunks, body, 0)

    def interleave(p, rank):
        pltpu.make_async_copy(
            gathered.at[pl.ds(0, TP - 1), p, pl.ds(rank * HALF, HALF)],
            gathered.at[pl.ds(0, TP - 1), p, pl.ds(rank * HALF, HALF)],
            recv_sem.at[p, rank],
        ).wait()
        for half in range(2):
            at = rank * HALF + half * 32
            for b in range(INNER // 256):
                columns = slice(b * 256, (b + 1) * 256)
                stacked = jnp.concatenate(
                    [gathered[g, p, at : at + 32, columns] for g in range(TP)], axis=0
                )
                first = (p * (length // TP) + at) * TP
                final[first : first + 256, columns] = dot(perm3[...], stacked).astype(BF16)

    pltpu.make_async_copy(gathered.at[me], gathered.at[me], own_sem).wait()
    for rank in range(3):
        interleave(0, rank)

    pltpu.make_async_copy(
        osend.at[pl.ds(0, 16 * (ns - 1))], osend.at[pl.ds(0, 16 * (ns - 1))], osend_sem
    ).wait()
    pltpu.make_async_copy(
        orecv.at[pl.ds(0, 16 * (ns - 1))], orecv.at[pl.ds(0, 16 * (ns - 1))], orecv_sem
    ).wait()
    table = dot_first(perm[...], orecv[...]).astype(BF16)
    for q in range(4):
        dec_out[:, q * 256 : (q + 1) * 256] = table[q * n64 : (q + 1) * n64]

    for rank in range(3):
        interleave(1, rank)
    for d in range(1, TP):
        peer = lax.rem(me + d, TP)
        pltpu.make_async_copy(gathered.at[peer], gathered.at[peer], send_sem.at[peer]).wait()


def per_device(
    ns,
    prompt_rows,
    prompt_dt,
    decode_rows,
    decode_dt,
    placement,
    conv_weight,
    conv_bias,
    dt_bias,
    a_log,
    skip_gain,
    norm_gain,
):
    length = prompt_rows.shape[1]
    chunks = length // SPAN
    n64, n256 = 4 * ns, 16 * ns
    vmem = pl.BlockSpec(memory_space=pltpu.VMEM)
    hbm = pl.BlockSpec(memory_space=pl.ANY)
    final, dec = pl.pallas_call(
        functools.partial(kernel, ns, length),
        out_shape=(
            pltpu.VMEM((2 * length, INNER), BF16),
            jax.ShapeDtypeStruct((n64, INNER), BF16),
        ),
        in_specs=[hbm, vmem, vmem, vmem, pl.BlockSpec(memory_space=pltpu.SMEM)] + [vmem] * 6,
        out_specs=(vmem, vmem),
        scratch_shapes=[
            pltpu.VMEM((TP, 2, length // TP, INNER), BF16),
            pltpu.VMEM((2, length, ROW), BF16),
            pltpu.VMEM((2, 16, XBC), BF16),
            pltpu.VMEM((length, INNER), F32),
            pltpu.VMEM((chunks, 4 * SPAN, INNER), BF16),
            pltpu.VMEM((chunks, SPAN, 2 * STATE), F32),
            pltpu.VMEM((chunks, 2 * HEADS, SPAN), BF16),
            pltpu.VMEM((chunks, 2 * HEADS, SPAN), BF16),
            pltpu.VMEM((chunks, 8, INNER), F32),
            pltpu.VMEM((2 * HEADS, INNER), BF16),
            pltpu.VMEM((SPAN, INNER), F32),
            pltpu.VMEM((SPAN, INNER), F32),
            pltpu.VMEM((2, STATE, INNER), F32),
            pltpu.VMEM((8, XBC), F32),
            pltpu.VMEM((1, INNER), F32),
            pltpu.VMEM((n256, n256), BF16),
            pltpu.VMEM((n256, n256), BF16),
            pltpu.VMEM((256, 256), BF16),
            pltpu.VMEM((n256, 640), BF16),
            pltpu.VMEM((n256, 640), BF16),
            pltpu.VMEM((n256, 640), BF16),
            pltpu.VMEM((n256, 640), F32),
            pltpu.VMEM((n256, 256), BF16),
            pltpu.VMEM((n256, 256), BF16),
            pltpu.SemaphoreType.DMA((2, chunks)),
            pltpu.SemaphoreType.DMA((TP,)),
            pltpu.SemaphoreType.DMA((2, 3)),
            pltpu.SemaphoreType.DMA,
            pltpu.SemaphoreType.DMA,
            pltpu.SemaphoreType.DMA,
            pltpu.SemaphoreType.DMA,
            pltpu.SemaphoreType.DMA,
        ],
        compiler_params=pltpu.CompilerParams(
            collective_id=0, has_side_effects=True, vmem_limit_bytes=52 * 2**20
        ),
    )(
        prompt_rows[:, :, 0, :],
        prompt_dt[:, :, 0, :].transpose(0, 2, 1),
        decode_rows[:, 0, :, 0, :].transpose(1, 0, 2),
        decode_dt[:, 0, :, 0, :].transpose(1, 2, 0),
        placement,
        conv_weight[0],
        conv_bias,
        dt_bias,
        a_log,
        skip_gain,
        norm_gain,
    )
    prefill_out = final.reshape(2, length // TP, TP, INNER)
    decode_out = dec.reshape(2, 2 * ns, INNER).transpose(1, 0, 2)
    return prefill_out, decode_out.reshape(2 * ns, 1, 2, 1, INNER)


def solution(mesh):
    in_specs = (
        P("samp", None, "tp", None),
        P("samp", None, "tp", None),
        P(None, "samp", None, "tp", None),
        P(None, "samp", None, "tp", None),
        P(),
        P("tp", None, None),
        P("tp", None),
        P("tp", None),
        P("tp", None),
        P("tp", None),
        P("tp", None),
    )
    out_specs = (P("samp", "tp", None, None), P(None, "samp", None, "tp", None))
    return jax.shard_map(
        functools.partial(per_device, mesh.shape["samp"]),
        mesh=mesh,
        in_specs=in_specs,
        out_specs=out_specs,
        check_vma=False,
    )
```

```python
import functools

import jax
import jax.numpy as jnp
from jax import lax
from jax.experimental import pallas as pl
from jax.experimental.pallas import tpu as pltpu
from jax.sharding import PartitionSpec as P

MESH = pl.DeviceIdType.MESH
HIGHEST = lax.Precision.HIGHEST
F32 = jnp.float32
BF16 = jnp.bfloat16
EPS = 1e-05

HEADS = 16
HEAD = 64
INNER = HEADS * HEAD
STATE = 128
XBC = INNER + 2 * STATE
ROW = XBC + INNER
SPAN = 128
HALF = SPAN // 2
TP = 8


def split(value):
    high = value.astype(BF16)
    return high, (value - high.astype(F32)).astype(BF16)


def silu_of_half(half):
    return half + half * jnp.tanh(half)


def softplus(value):
    return jnp.maximum(value, 0.0) + jnp.log1p(jnp.exp(-jnp.abs(value)))


def dot(left, right, precision=None):
    return jnp.dot(left, right, preferred_element_type=F32, precision=precision)


def dot_first(left, right):
    return lax.dot_general(left, right, (((0,), (0,)), ((), ())), preferred_element_type=F32)


def dot_last(left, right, precision=None):
    return lax.dot_general(
        left, right, (((1,), (1,)), ((), ())), preferred_element_type=F32, precision=precision
    )


def iota(shape, axis):
    return lax.broadcasted_iota(jnp.int32, shape, axis)


def kernel(
    ns,
    length,
    rows_hbm,
    raw_dt,
    drows,
    ddt,
    placement,
    conv_w,
    conv_b,
    dt_bias,
    a_log,
    skip_gain,
    norm_gain,
    final,
    dec_out,
    gathered,
    rows,
    carry,
    xs,
    mats,
    bcs,
    fac_in,
    fac_out,
    ends,
    expand,
    fx,
    gated,
    state,
    halfw,
    skip,
    perm,
    perm2,
    perm3,
    dpieces,
    dsend,
    drecv,
    dtable,
    osend,
    orecv,
    in_sem,
    send_sem,
    recv_sem,
    own_sem,
    dsend_sem,
    drecv_sem,
    osend_sem,
    orecv_sem,
):
    me = lax.axis_index("tp")
    sm = lax.axis_index("samp")
    x0 = me // 2
    chunks = length // SPAN
    n256 = 16 * ns

    def rows_in(p, c):
        part = pl.ds(pl.multiple_of(c * SPAN, SPAN), SPAN)
        return pltpu.make_async_copy(rows_hbm.at[p, part], rows.at[p, part], in_sem.at[p, c])

    for p in range(2):
        lax.fori_loop(0, chunks, lambda c, _: (rows_in(p, c).start(), 0)[1], 0)

    barrier = pltpu.get_barrier_semaphore()
    for d in range(1, TP):
        pl.semaphore_signal(
            barrier, inc=1, device_id={"tp": lax.rem(me + d, TP)}, device_id_type=MESH
        )
    for d in range(1, ns):
        pl.semaphore_signal(
            barrier, inc=1, device_id={"samp": lax.rem(sm + d, ns)}, device_id_type=MESH
        )

    halfw[0:4, :] = conv_w[...] * 0.5
    halfw[4:5, :] = conv_b[...] * 0.5
    eye = iota((HEADS, HEADS), 0) == iota((HEADS, HEADS), 1)

    def column(row):
        return jnp.sum(jnp.where(eye, row, 0.0), axis=1, keepdims=True)

    bias_row = dt_bias[...]
    rate_row = -jnp.exp(a_log[...])
    bias_col = column(bias_row)
    rate_col = column(rate_row)
    own = (iota((HEADS, INNER), 0) == iota((HEADS, INNER), 1) // HEAD).astype(F32)
    expand[0:HEADS, :] = own.astype(BF16)
    expand[HEADS : 2 * HEADS, :] = own.astype(BF16)
    skip[...] = jnp.sum(own * column(skip_gain[...]), axis=0, keepdims=True)

    def prepare(p):
        upper = (iota((SPAN, SPAN), 0) <= iota((SPAN, SPAN), 1)).astype(F32)
        step = softplus(raw_dt[p].astype(F32) + bias_col)
        steps = jnp.concatenate([step[:, c * SPAN : (c + 1) * SPAN] for c in range(chunks)], axis=0)
        decay = steps * jnp.concatenate([rate_col] * chunks, axis=0)
        total = dot(decay, upper, HIGHEST)
        middle = 0.5 * total[:, SPAN - 1 : SPAN]
        from_middle = total - middle
        in_high, in_low = split(jnp.exp(-from_middle) * steps)
        out_high, out_low = split(jnp.exp(from_middle))
        for c in range(chunks):
            part = slice(c * HEADS, (c + 1) * HEADS)
            fac_in[c, 0:HEADS, :] = in_high[part]
            fac_in[c, HEADS : 2 * HEADS, :] = in_low[part]
            fac_out[c, 0:HEADS, :] = out_high[part]
            fac_out[c, HEADS : 2 * HEADS, :] = out_low[part]
            ends[c] = jnp.broadcast_to(
                jnp.sum(own * jnp.exp(middle[part]), axis=0, keepdims=True), (8, INNER)
            )

    n64 = 4 * ns
    n32 = 2 * ns

    def block_of(k):
        return pl.ds(pl.multiple_of(16 * k, 16), 16)

    def to_holder(d):
        peer = lax.rem(sm + d, ns)
        return pltpu.make_async_remote_copy(
            src_ref=dsend.at[block_of(peer)],
            dst_ref=drecv.at[block_of(sm)],
            send_sem=dsend_sem,
            recv_sem=drecv_sem,
            device_id={"samp": peer},
            device_id_type=MESH,
        )

    def sort_decode_rows():
        lanes = iota((1, n256), 1)
        slot_of = jnp.zeros((1, n256), jnp.int32)
        for prompt in range(n32):
            slot_of = jnp.where(lanes % n32 == prompt, placement[prompt], slot_of)
        r = iota((n256, n256), 0)
        s = iota((n256, n256), 1)
        perm[...] = jnp.where(
            ((r // 4) % 4 == s // n64)
            & (slot_of == 2 * (r // 16) + (r // 2) % 2)
            & (r % 2 == (s // n32) % 2),
            1.0,
            0.0,
        ).astype(BF16)
        perm2[...] = jnp.where(
            (r // n64 == (s // 4) % 4) & ((r // ns) % 4 == s % 4) & (r % ns == s // 16), 1.0, 0.0
        ).astype(BF16)
        r = iota((256, 256), 0)
        s = iota((256, 256), 1)
        perm3[...] = jnp.where((r % TP == s // 32) & (r // TP == s % 32), 1.0, 0.0).astype(BF16)
        unit = jnp.where(iota((n32, n32), 0) == iota((n32, n32), 1), 1.0, 0.0).astype(BF16)
        dpieces[...] = jnp.zeros_like(dpieces)
        for i in range(2):
            for q in range(4):
                part = slice(q * n64 + i * n32, q * n64 + (i + 1) * n32)
                dpieces[part, 0:512] = drows[:, i, q * 512 : (q + 1) * 512]
                if q < 2:
                    dpieces[part, 512:640] = drows[:, i, 2048 + q * 128 : 2176 + q * 128]
                if q == 2:
                    dpieces[part, 512 : 512 + HEADS] = dot_last(unit, ddt[i]).astype(BF16)
        dsend[...] = dot(perm[...], dpieces[...]).astype(BF16)
        drecv[block_of(sm), :] = dsend[block_of(sm), :]

    def conv_half(now, last, columns):
        both = jnp.concatenate([last, now], axis=0)
        result = halfw[4:5, columns] + halfw[3:4, columns] * now
        for back in range(1, 4):
            result = result + halfw[3 - back : 4 - back, columns] * pltpu.roll(both, back, 0)[8:]
        return result

    def first_pass(p, c):
        rows_in(p, c).wait()
        base = pl.multiple_of(c * SPAN, SPAN)
        part = pl.ds(base, SPAN)
        keep = jnp.where(c > 0, 1.0, 0.0).astype(F32)
        fx[...] = dot_first(fac_in[c], expand[...])
        for b in range(XBC // 128):
            columns = slice(b * 128, (b + 1) * 128)
            now = rows[p, part, columns].astype(F32)
            last = carry[p, :, columns].astype(F32)[8:16] * keep
            value = silu_of_half(conv_half(now, last, columns))
            if b < INNER // 128:
                xs[part, columns] = value
                high, low = split(value * fx[:, columns])
                mats[c, 0:128, columns] = low
                mats[c, 128:256, columns] = high
            else:
                bcs[c, :, b * 128 - INNER : (b + 1) * 128 - INNER] = value
        carry[p] = rows[p, pl.ds(pl.multiple_of(base + SPAN - 16, 16), 16), 0:XBC]
        b_high, b_low = split(bcs[c, :, 0:128].T)
        b_twice = jnp.concatenate([b_high, b_high], axis=1)
        for b in range(INNER // 256):
            columns = slice(b * 256, (b + 1) * 256)
            end = ends[c, 0:1, columns]
            entering = state[p, :, columns] * end
            high, low = split(entering)
            mats[c, 256:384, columns] = high
            mats[c, 384:512, columns] = low
            added = dot(b_twice, mats[c, 0:256, columns]) + dot(b_low, mats[c, 128:256, columns])
            state[p, :, columns] = end * (added + entering)

    def second_pass(p, unit, third):
        c = 3 * unit + third
        base = pl.multiple_of(c * SPAN, SPAN)
        part = pl.ds(base, SPAN)
        fx[...] = dot_first(fac_out[c], expand[...])
        b_now = bcs[c, :, 0:128]
        c_now = bcs[c, :, 128:256]
        scores = dot_last(c_now, b_now, HIGHEST)
        scores = jnp.where(iota((SPAN, SPAN), 0) >= iota((SPAN, SPAN), 1), scores, 0.0)
        s_high, s_low = split(scores)
        c_high, c_low = split(c_now)
        left = jnp.concatenate([s_high, s_high, c_high, c_high], axis=1)
        left_low = jnp.concatenate([s_low, c_low], axis=1)
        squares = jnp.zeros((SPAN, 128), F32)
        for b in range(INNER // 256):
            columns = slice(b * 256, (b + 1) * 256)
            y = dot(left, mats[c, :, columns]) + dot(left_low, mats[c, 128:384, columns])
            y = fx[:, columns] * y + skip[:, columns] * xs[part, columns]
            z_half = 0.5 * rows[p, part, XBC + b * 256 : XBC + (b + 1) * 256].astype(F32)
            g = y * silu_of_half(z_half)
            gated[:, columns] = g
            squares = squares + g[:, 0:128] * g[:, 0:128] + g[:, 128:256] * g[:, 128:256]
        mean = jnp.sum(squares, axis=1, keepdims=True) * (1.0 / INNER)
        scale = lax.rsqrt(mean + EPS)
        for b in range(INNER // 128):
            columns = slice(b * 128, (b + 1) * 128)
            rows[p, part, columns] = (gated[:, columns] * scale * norm_gain[:, columns]).astype(BF16)
        for half in range(2):
            piece = 2 * third + half
            dest = 2 * unit + piece // 3
            rank = lax.rem(piece, 3)
            source = rows.at[p, pl.ds(pl.multiple_of(base + half * HALF, HALF), HALF), pl.ds(0, INNER)]
            target = gathered.at[me, p, pl.ds(pl.multiple_of(rank * HALF, HALF), HALF)]

            @pl.when(dest != me)
            def _():
                pltpu.make_async_remote_copy(
                    src_ref=source,
                    dst_ref=target,
                    send_sem=send_sem.at[dest],
                    recv_sem=recv_sem.at[p, rank],
                    device_id={"tp": dest},
                    device_id_type=MESH,
                ).start()

            @pl.when(dest == me)
            def _():
                pltpu.make_async_copy(source, target, own_sem).start()

    def decode():
        for d in range(1, ns):
            to_holder(d).wait_send()
        pltpu.make_async_copy(
            drecv.at[pl.ds(0, 16 * (ns - 1))], drecv.at[pl.ds(0, 16 * (ns - 1))], drecv_sem
        ).wait()
        dtable[...] = dot(perm2[...], drecv[...])
        pieces = []
        for j in range(2):
            tail = carry[j].astype(F32)
            window = [tail[13:14], tail[14:15], tail[15:16]]
            gates, steps = [], []
            for i in range(2):
                at = [slice(q * n64 + (2 * j + i) * ns, q * n64 + (2 * j + i + 1) * ns) for q in range(4)]
                window.append(
                    jnp.concatenate(
                        [dtable[at[0], 0:512], dtable[at[1], 0:512], dtable[at[2], 0:256]], axis=1
                    )
                )
                gates.append(
                    jnp.concatenate(
                        [
                            dtable[at[2], 256:512],
                            dtable[at[3], 0:512],
                            dtable[at[0], 512:640],
                            dtable[at[1], 512:640],
                        ],
                        axis=1,
                    )
                )
                steps.append(softplus(dtable[at[2], 512 : 512 + HEADS] + bias_row))
            convs = []
            for i in range(2):
                half = halfw[4:5, :]
                for tap in range(4):
                    half = half + halfw[tap : tap + 1, :] * window[i + tap]
                convs.append(silu_of_half(half))
            x = [v[:, 0:INNER] for v in convs]
            b = [v[:, INNER : INNER + STATE] for v in convs]
            cc = [v[:, INNER + STATE : XBC] for v in convs]
            from_state = dot(jnp.concatenate(cc, axis=0), state[j], HIGHEST)
            wide_dt = [dot(v, own, HIGHEST) for v in steps]
            wide_decay = [dot(jnp.exp(v * rate_row), own, HIGHEST) for v in steps]

            def over(i, k):
                return jnp.sum(b[i] * cc[k], axis=1, keepdims=True)

            first = wide_dt[0] * x[0]
            second = wide_dt[1] * x[1]
            y = [
                wide_decay[0] * from_state[0:ns] + first * over(0, 0) + skip[...] * x[0],
                wide_decay[1] * (wide_decay[0] * from_state[ns : 2 * ns] + first * over(0, 1))
                + second * over(1, 1)
                + skip[...] * x[1],
            ]
            for i in range(2):
                g = y[i] * silu_of_half(0.5 * gates[i])
                scale = lax.rsqrt(jnp.sum(g * g, axis=1, keepdims=True) * (1.0 / INNER) + EPS)
                pieces.append((g * scale * norm_gain[...]).astype(BF16))
        table = jnp.concatenate(
            [v[:, q * 256 : (q + 1) * 256] for q in range(4) for v in pieces], axis=0
        )
        osend[...] = dot_first(perm2[...], table).astype(BF16)

        for d in range(1, ns):
            to_sample(d).start()
        orecv[block_of(sm), :] = osend[block_of(sm), :]

    def to_sample(d):
        peer = lax.rem(sm + d, ns)
        return pltpu.make_async_remote_copy(
            src_ref=osend.at[block_of(peer)],
            dst_ref=orecv.at[block_of(sm)],
            send_sem=osend_sem,
            recv_sem=orecv_sem,
            device_id={"samp": peer},
            device_id_type=MESH,
        )

    state[...] = jnp.zeros_like(state)
    carry[...] = jnp.zeros_like(carry)
    prepare(0)
    lead = 4
    lax.fori_loop(0, lead, lambda c, _: (first_pass(0, c), 0)[1], 0)
    pl.semaphore_wait(barrier, TP - 1 + ns - 1)
    edge = (x0 == 0) | (x0 == 3)
    one = jnp.where(edge, 0, 2)
    two = jnp.where(lax.rem(x0, 2) == 0, 1, jnp.where(x0 == 1, 0, 2))
    low = jnp.minimum(one, two)
    high = jnp.maximum(one, two)

    def body(t, _):
        p = t // (2 * chunks)
        u = lax.rem(t, 2 * chunks)
        lone = (p == 0) & ((u == lead) | (u == 10))
        is_first = jnp.where(p == 0, u < chunks + 2, u < chunks) & jnp.logical_not(lone)

        @pl.when(t == 2 * chunks)
        def _():
            prepare(1)

        @pl.when(is_first)
        def _():
            first_pass(p, jnp.where(p == 0, u - 1 - jnp.where(u > 10, 1, 0), u))

        @pl.when(jnp.logical_not(is_first))
        def _():
            later = u - chunks - 2
            later = later + jnp.where(later >= low, 1, 0)
            later = later + jnp.where(later >= high, 1, 0)
            k = jnp.where(u == lead, one, jnp.where(u == 10, two, later))
            k = jnp.where(p == 0, k, u - chunks)
            lane = lax.rem(k, 4)
            unit = lax.rem(x0 + 1 + lane, 4)
            row = k // 4
            second_pass(p, unit, jnp.where(lax.rem(lane + p, 2) == 0, row, 2 - row))

        @pl.when(t == lead)
        def _():
            sort_decode_rows()
            for d in range(1, ns):
                to_holder(d).start()

        @pl.when(t == 3 * chunks - 1)
        def _():
            decode()

        return 0

    lax.fori_loop(lead, 4 * chunks, body, 0)

    def interleave(p, rank):
        pltpu.make_async_copy(
            gathered.at[pl.ds(0, TP - 1), p, pl.ds(rank * HALF, HALF)],
            gathered.at[pl.ds(0, TP - 1), p, pl.ds(rank * HALF, HALF)],
            recv_sem.at[p, rank],
        ).wait()
        for half in range(2):
            at = pl.multiple_of(rank * HALF + half * 32, 32)
            for b in range(INNER // 256):
                columns = slice(b * 256, (b + 1) * 256)
                stacked = jnp.concatenate(
                    [gathered[g, p, pl.ds(at, 32), columns] for g in range(TP)], axis=0
                )
                first = pl.multiple_of((p * (length // TP) + at) * TP, 256)
                final[pl.ds(first, 256), columns] = dot(perm3[...], stacked).astype(BF16)

    pltpu.make_async_copy(gathered.at[me], gathered.at[me], own_sem).wait()
    lax.fori_loop(0, 3, lambda i, _: (interleave(0, i), 0)[1], 0)

    pltpu.make_async_copy(
        osend.at[pl.ds(0, 16 * (ns - 1))], osend.at[pl.ds(0, 16 * (ns - 1))], osend_sem
    ).wait()
    pltpu.make_async_copy(
        orecv.at[pl.ds(0, 16 * (ns - 1))], orecv.at[pl.ds(0, 16 * (ns - 1))], orecv_sem
    ).wait()
    table = dot_first(perm[...], orecv[...]).astype(BF16)
    for q in range(4):
        for i in range(2):
            part = table[q * n64 + i * n32 : q * n64 + (i + 1) * n32]
            dec_out[:, i, q * 256 : (q + 1) * 256] = part

    turn = 2 - 2 * lax.rem(me, 2)
    lax.fori_loop(0, 3, lambda i, _: (interleave(1, lax.rem(i + turn, 3)), 0)[1], 0)
    for d in range(1, TP):
        peer = lax.rem(me + d, TP)
        pltpu.make_async_copy(gathered.at[peer], gathered.at[peer], send_sem.at[peer]).wait()


def per_device(
    ns,
    prompt_rows,
    prompt_dt,
    decode_rows,
    decode_dt,
    placement,
    conv_weight,
    conv_bias,
    dt_bias,
    a_log,
    skip_gain,
    norm_gain,
):
    length = prompt_rows.shape[1]
    chunks = length // SPAN
    n64, n256 = 4 * ns, 16 * ns
    vmem = pl.BlockSpec(memory_space=pltpu.VMEM)
    hbm = pl.BlockSpec(memory_space=pl.ANY)
    final, dec = pl.pallas_call(
        functools.partial(kernel, ns, length),
        out_shape=(
            pltpu.VMEM((2 * length, INNER), BF16),
            pltpu.VMEM((2 * ns, 2, INNER), BF16),
        ),
        in_specs=[hbm, vmem, vmem, vmem, pl.BlockSpec(memory_space=pltpu.SMEM)] + [vmem] * 6,
        out_specs=(vmem, vmem),
        scratch_shapes=[
            pltpu.VMEM((TP, 2, length // TP, INNER), BF16),
            pltpu.VMEM((2, length, ROW), BF16),
            pltpu.VMEM((2, 16, XBC), BF16),
            pltpu.VMEM((length, INNER), F32),
            pltpu.VMEM((chunks, 4 * SPAN, INNER), BF16),
            pltpu.VMEM((chunks, SPAN, 2 * STATE), F32),
            pltpu.VMEM((chunks, 2 * HEADS, SPAN), BF16),
            pltpu.VMEM((chunks, 2 * HEADS, SPAN), BF16),
            pltpu.VMEM((chunks, 8, INNER), F32),
            pltpu.VMEM((2 * HEADS, INNER), BF16),
            pltpu.VMEM((SPAN, INNER), F32),
            pltpu.VMEM((SPAN, INNER), F32),
            pltpu.VMEM((2, STATE, INNER), F32),
            pltpu.VMEM((8, XBC), F32),
            pltpu.VMEM((1, INNER), F32),
            pltpu.VMEM((n256, n256), BF16),
            pltpu.VMEM((n256, n256), BF16),
            pltpu.VMEM((256, 256), BF16),
            pltpu.VMEM((n256, 640), BF16),
            pltpu.VMEM((n256, 640), BF16),
            pltpu.VMEM((n256, 640), BF16),
            pltpu.VMEM((n256, 640), F32),
            pltpu.VMEM((n256, 256), BF16),
            pltpu.VMEM((n256, 256), BF16),
            pltpu.SemaphoreType.DMA((2, chunks)),
            pltpu.SemaphoreType.DMA((TP,)),
            pltpu.SemaphoreType.DMA((2, 3)),
            pltpu.SemaphoreType.DMA,
            pltpu.SemaphoreType.DMA,
            pltpu.SemaphoreType.DMA,
            pltpu.SemaphoreType.DMA,
            pltpu.SemaphoreType.DMA,
        ],
        compiler_params=pltpu.CompilerParams(
            collective_id=0, has_side_effects=True, vmem_limit_bytes=52 * 2**20
        ),
    )(
        prompt_rows[:, :, 0, :],
        prompt_dt[:, :, 0, :].transpose(0, 2, 1),
        decode_rows[:, 0, :, 0, :],
        decode_dt[:, 0, :, 0, :].transpose(1, 2, 0),
        placement,
        conv_weight[0],
        conv_bias,
        dt_bias,
        a_log,
        skip_gain,
        norm_gain,
    )
    prefill_out = final.reshape(2, length // TP, TP, INNER)
    return prefill_out, dec.reshape(2 * ns, 1, 2, 1, INNER)


def solution(mesh):
    in_specs = (
        P("samp", None, "tp", None),
        P("samp", None, "tp", None),
        P(None, "samp", None, "tp", None),
        P(None, "samp", None, "tp", None),
        P(),
        P("tp", None, None),
        P("tp", None),
        P("tp", None),
        P("tp", None),
        P("tp", None),
        P("tp", None),
    )
    out_specs = (P("samp", "tp", None, None), P(None, "samp", None, "tp", None))
    return jax.shard_map(
        functools.partial(per_device, mesh.shape["samp"]),
        mesh=mesh,
        in_specs=in_specs,
        out_specs=out_specs,
        check_vma=False,
    )
```

```python
import functools

import jax
import jax.numpy as jnp
from jax import lax
from jax.experimental import pallas as pl
from jax.experimental.pallas import tpu as pltpu
from jax.sharding import PartitionSpec as P

MESH = pl.DeviceIdType.MESH
HIGHEST = lax.Precision.HIGHEST
F32 = jnp.float32
BF16 = jnp.bfloat16
EPS = 1e-05

HEADS = 16
HEAD = 64
INNER = HEADS * HEAD
STATE = 128
XBC = INNER + 2 * STATE
ROW = XBC + INNER
SPAN = 128
HALF = SPAN // 2
TP = 8


def split(value):
    high = value.astype(BF16)
    return high, (value - high.astype(F32)).astype(BF16)


def silu_of_half(half):
    return half + half * jnp.tanh(half)


def softplus(value):
    return jnp.maximum(value, 0.0) + jnp.log1p(jnp.exp(-jnp.abs(value)))


def dot(left, right, precision=None):
    return jnp.dot(left, right, preferred_element_type=F32, precision=precision)


def dot_first(left, right):
    return lax.dot_general(left, right, (((0,), (0,)), ((), ())), preferred_element_type=F32)


def dot_last(left, right, precision=None):
    return lax.dot_general(
        left, right, (((1,), (1,)), ((), ())), preferred_element_type=F32, precision=precision
    )


def iota(shape, axis):
    return lax.broadcasted_iota(jnp.int32, shape, axis)


def kernel(
    ns,
    length,
    rows_hbm,
    raw_dt,
    drows,
    ddt,
    placement,
    conv_w,
    conv_b,
    dt_bias,
    a_log,
    skip_gain,
    norm_gain,
    final,
    dec_out,
    gathered,
    rows,
    carry,
    xs,
    mats,
    bcs,
    fac_in,
    fac_out,
    ends,
    expand,
    fx,
    gated,
    state,
    halfw,
    skip,
    perm,
    perm2,
    perm3,
    dpieces,
    dsend,
    drecv,
    dtable,
    osend,
    orecv,
    in_sem,
    send_sem,
    recv_sem,
    own_sem,
    dsend_sem,
    drecv_sem,
    osend_sem,
    orecv_sem,
):
    me = lax.axis_index("tp")
    sm = lax.axis_index("samp")
    x0 = me // 2
    chunks = length // SPAN
    n256 = 16 * ns

    def rows_in(p, c):
        part = pl.ds(pl.multiple_of(c * SPAN, SPAN), SPAN)
        return pltpu.make_async_copy(rows_hbm.at[p, part], rows.at[p, part], in_sem.at[p, c])

    for p in range(2):
        lax.fori_loop(0, chunks, lambda c, _: (rows_in(p, c).start(), 0)[1], 0)

    barrier = pltpu.get_barrier_semaphore()
    for d in range(1, TP):
        pl.semaphore_signal(
            barrier, inc=1, device_id={"tp": lax.rem(me + d, TP)}, device_id_type=MESH
        )
    for d in range(1, ns):
        pl.semaphore_signal(
            barrier, inc=1, device_id={"samp": lax.rem(sm + d, ns)}, device_id_type=MESH
        )

    halfw[0:4, :] = conv_w[...] * 0.5
    halfw[4:5, :] = conv_b[...] * 0.5
    eye = iota((HEADS, HEADS), 0) == iota((HEADS, HEADS), 1)

    def column(row):
        return jnp.sum(jnp.where(eye, row, 0.0), axis=1, keepdims=True)

    bias_row = dt_bias[...]
    rate_row = -jnp.exp(a_log[...])
    bias_col = column(bias_row)
    rate_col = column(rate_row)
    own = (iota((HEADS, INNER), 0) == iota((HEADS, INNER), 1) // HEAD).astype(F32)
    expand[0:HEADS, :] = own.astype(BF16)
    expand[HEADS : 2 * HEADS, :] = own.astype(BF16)
    skip[...] = jnp.sum(own * column(skip_gain[...]), axis=0, keepdims=True)

    def prepare(p):
        upper = (iota((SPAN, SPAN), 0) <= iota((SPAN, SPAN), 1)).astype(F32)
        step = softplus(raw_dt[p].astype(F32) + bias_col)
        steps = jnp.concatenate([step[:, c * SPAN : (c + 1) * SPAN] for c in range(chunks)], axis=0)
        decay = steps * jnp.concatenate([rate_col] * chunks, axis=0)
        total = dot(decay, upper, HIGHEST)
        middle = 0.5 * total[:, SPAN - 1 : SPAN]
        from_middle = total - middle
        in_high, in_low = split(jnp.exp(-from_middle) * steps)
        out_high, out_low = split(jnp.exp(from_middle))
        for c in range(chunks):
            part = slice(c * HEADS, (c + 1) * HEADS)
            fac_in[c, 0:HEADS, :] = in_high[part]
            fac_in[c, HEADS : 2 * HEADS, :] = in_low[part]
            fac_out[c, 0:HEADS, :] = out_high[part]
            fac_out[c, HEADS : 2 * HEADS, :] = out_low[part]
            ends[c] = jnp.broadcast_to(
                jnp.sum(own * jnp.exp(middle[part]), axis=0, keepdims=True), (8, INNER)
            )

    n64 = 4 * ns
    n32 = 2 * ns

    def block_of(k):
        return pl.ds(pl.multiple_of(16 * k, 16), 16)

    def to_holder(d):
        peer = lax.rem(sm + d, ns)
        return pltpu.make_async_remote_copy(
            src_ref=dsend.at[block_of(peer)],
            dst_ref=drecv.at[block_of(sm)],
            send_sem=dsend_sem,
            recv_sem=drecv_sem,
            device_id={"samp": peer},
            device_id_type=MESH,
        )

    def order_tables():
        r = iota((n256, n256), 0)
        s = iota((n256, n256), 1)
        perm2[...] = jnp.where(
            (r // n64 == (s // 4) % 4) & ((r // ns) % 4 == s % 4) & (r % ns == s // 16), 1.0, 0.0
        ).astype(BF16)
        r = iota((256, 256), 0)
        s = iota((256, 256), 1)
        perm3[...] = jnp.where((r % TP == s // 32) & (r // TP == s % 32), 1.0, 0.0).astype(BF16)

    def sort_decode_rows():
        lanes = iota((1, n256), 1)
        slot_of = jnp.zeros((1, n256), jnp.int32)
        for prompt in range(n32):
            slot_of = jnp.where(lanes % n32 == prompt, placement[prompt], slot_of)
        r = iota((n256, n256), 0)
        s = iota((n256, n256), 1)
        perm[...] = jnp.where(
            ((r // 4) % 4 == s // n64)
            & (slot_of == 2 * (r // 16) + (r // 2) % 2)
            & (r % 2 == (s // n32) % 2),
            1.0,
            0.0,
        ).astype(BF16)
        unit = jnp.where(iota((n32, n32), 0) == iota((n32, n32), 1), 1.0, 0.0).astype(BF16)
        dpieces[...] = jnp.zeros_like(dpieces)
        for i in range(2):
            for q in range(4):
                part = slice(q * n64 + i * n32, q * n64 + (i + 1) * n32)
                dpieces[part, 0:512] = drows[:, i, q * 512 : (q + 1) * 512]
                if q < 2:
                    dpieces[part, 512:640] = drows[:, i, 2048 + q * 128 : 2176 + q * 128]
                if q == 2:
                    dpieces[part, 512 : 512 + HEADS] = dot_last(unit, ddt[i]).astype(BF16)
        dsend[...] = dot(perm[...], dpieces[...]).astype(BF16)
        drecv[block_of(sm), :] = dsend[block_of(sm), :]

    def conv_half(now, last, columns):
        both = jnp.concatenate([last, now], axis=0)
        result = halfw[4:5, columns] + halfw[3:4, columns] * now
        for back in range(1, 4):
            result = result + halfw[3 - back : 4 - back, columns] * pltpu.roll(both, back, 0)[8:]
        return result

    def first_pass(p, c):
        rows_in(p, c).wait()
        base = pl.multiple_of(c * SPAN, SPAN)
        part = pl.ds(base, SPAN)
        keep = jnp.where(c > 0, 1.0, 0.0).astype(F32)
        fx[...] = dot_first(fac_in[c], expand[...])
        for b in range(XBC // 128):
            columns = slice(b * 128, (b + 1) * 128)
            now = rows[p, part, columns].astype(F32)
            last = carry[p, :, columns].astype(F32)[8:16] * keep
            value = silu_of_half(conv_half(now, last, columns))
            if b < INNER // 128:
                xs[part, columns] = value
                high, low = split(value * fx[:, columns])
                mats[c, 0:128, columns] = low
                mats[c, 128:256, columns] = high
            else:
                bcs[c, :, b * 128 - INNER : (b + 1) * 128 - INNER] = value
        carry[p] = rows[p, pl.ds(pl.multiple_of(base + SPAN - 16, 16), 16), 0:XBC]
        b_high, b_low = split(bcs[c, :, 0:128].T)
        b_twice = jnp.concatenate([b_high, b_high], axis=1)
        for b in range(INNER // 256):
            columns = slice(b * 256, (b + 1) * 256)
            end = ends[c, 0:1, columns]
            entering = state[p, :, columns] * end
            high, low = split(entering)
            mats[c, 256:384, columns] = high
            mats[c, 384:512, columns] = low
            added = dot(b_twice, mats[c, 0:256, columns]) + dot(b_low, mats[c, 128:256, columns])
            state[p, :, columns] = end * (added + entering)

    def second_pass(p, unit, third):
        c = 3 * unit + third
        base = pl.multiple_of(c * SPAN, SPAN)
        part = pl.ds(base, SPAN)
        fx[...] = dot_first(fac_out[c], expand[...])
        b_now = bcs[c, :, 0:128]
        c_now = bcs[c, :, 128:256]
        scores = dot_last(c_now, b_now, HIGHEST)
        scores = jnp.where(iota((SPAN, SPAN), 0) >= iota((SPAN, SPAN), 1), scores, 0.0)
        s_high, s_low = split(scores)
        c_high, c_low = split(c_now)
        left = jnp.concatenate([s_high, s_high, c_high, c_high], axis=1)
        left_low = jnp.concatenate([s_low, c_low], axis=1)
        squares = jnp.zeros((SPAN, 128), F32)
        for b in range(INNER // 256):
            columns = slice(b * 256, (b + 1) * 256)
            y = dot(left, mats[c, :, columns]) + dot(left_low, mats[c, 128:384, columns])
            y = fx[:, columns] * y + skip[:, columns] * xs[part, columns]
            z_half = 0.5 * rows[p, part, XBC + b * 256 : XBC + (b + 1) * 256].astype(F32)
            g = y * silu_of_half(z_half)
            gated[:, columns] = g
            squares = squares + g[:, 0:128] * g[:, 0:128] + g[:, 128:256] * g[:, 128:256]
        mean = jnp.sum(squares, axis=1, keepdims=True) * (1.0 / INNER)
        scale = lax.rsqrt(mean + EPS)
        for b in range(INNER // 128):
            columns = slice(b * 128, (b + 1) * 128)
            rows[p, part, columns] = (gated[:, columns] * scale * norm_gain[:, columns]).astype(BF16)
        for half in range(2):
            piece = 2 * third + half
            dest = 2 * unit + piece // 3
            rank = lax.rem(piece, 3)
            source = rows.at[p, pl.ds(pl.multiple_of(base + half * HALF, HALF), HALF), pl.ds(0, INNER)]
            target = gathered.at[me, p, pl.ds(pl.multiple_of(rank * HALF, HALF), HALF)]

            @pl.when(dest != me)
            def _():
                pltpu.make_async_remote_copy(
                    src_ref=source,
                    dst_ref=target,
                    send_sem=send_sem.at[dest],
                    recv_sem=recv_sem.at[p, rank],
                    device_id={"tp": dest},
                    device_id_type=MESH,
                ).start()

            @pl.when(dest == me)
            def _():
                pltpu.make_async_copy(source, target, own_sem).start()

    def decode():
        for d in range(1, ns):
            to_holder(d).wait_send()
        pltpu.make_async_copy(
            drecv.at[pl.ds(0, 16 * (ns - 1))], drecv.at[pl.ds(0, 16 * (ns - 1))], drecv_sem
        ).wait()
        dtable[...] = dot(perm2[...], drecv[...])
        pieces = []
        for j in range(2):
            tail = carry[j].astype(F32)
            window = [tail[13:14], tail[14:15], tail[15:16]]
            gates, steps = [], []
            for i in range(2):
                at = [slice(q * n64 + (2 * j + i) * ns, q * n64 + (2 * j + i + 1) * ns) for q in range(4)]
                window.append(
                    jnp.concatenate(
                        [dtable[at[0], 0:512], dtable[at[1], 0:512], dtable[at[2], 0:256]], axis=1
                    )
                )
                gates.append(
                    jnp.concatenate(
                        [
                            dtable[at[2], 256:512],
                            dtable[at[3], 0:512],
                            dtable[at[0], 512:640],
                            dtable[at[1], 512:640],
                        ],
                        axis=1,
                    )
                )
                steps.append(softplus(dtable[at[2], 512 : 512 + HEADS] + bias_row))
            convs = []
            for i in range(2):
                half = halfw[4:5, :]
                for tap in range(4):
                    half = half + halfw[tap : tap + 1, :] * window[i + tap]
                convs.append(silu_of_half(half))
            x = [v[:, 0:INNER] for v in convs]
            b = [v[:, INNER : INNER + STATE] for v in convs]
            cc = [v[:, INNER + STATE : XBC] for v in convs]
            from_state = dot(jnp.concatenate(cc, axis=0), state[j], HIGHEST)
            wide_dt = [dot(v, own, HIGHEST) for v in steps]
            wide_decay = [dot(jnp.exp(v * rate_row), own, HIGHEST) for v in steps]

            def over(i, k):
                return jnp.sum(b[i] * cc[k], axis=1, keepdims=True)

            first = wide_dt[0] * x[0]
            second = wide_dt[1] * x[1]
            y = [
                wide_decay[0] * from_state[0:ns] + first * over(0, 0) + skip[...] * x[0],
                wide_decay[1] * (wide_decay[0] * from_state[ns : 2 * ns] + first * over(0, 1))
                + second * over(1, 1)
                + skip[...] * x[1],
            ]
            for i in range(2):
                g = y[i] * silu_of_half(0.5 * gates[i])
                scale = lax.rsqrt(jnp.sum(g * g, axis=1, keepdims=True) * (1.0 / INNER) + EPS)
                pieces.append((g * scale * norm_gain[...]).astype(BF16))
        table = jnp.concatenate(
            [v[:, q * 256 : (q + 1) * 256] for q in range(4) for v in pieces], axis=0
        )
        osend[...] = dot_first(perm2[...], table).astype(BF16)

        for d in range(1, ns):
            to_sample(d).start()
        orecv[block_of(sm), :] = osend[block_of(sm), :]

    def to_sample(d):
        peer = lax.rem(sm + d, ns)
        return pltpu.make_async_remote_copy(
            src_ref=osend.at[block_of(peer)],
            dst_ref=orecv.at[block_of(sm)],
            send_sem=osend_sem,
            recv_sem=orecv_sem,
            device_id={"samp": peer},
            device_id_type=MESH,
        )

    state[...] = jnp.zeros_like(state)
    carry[...] = jnp.zeros_like(carry)
    prepare(0)
    lead = 4
    lax.fori_loop(0, lead, lambda c, _: (first_pass(0, c), 0)[1], 0)
    pl.semaphore_wait(barrier, TP - 1 + ns - 1)
    edge = (x0 == 0) | (x0 == 3)
    one = jnp.where(edge, 0, 2)
    two = jnp.where(lax.rem(x0, 2) == 0, 1, jnp.where(x0 == 1, 0, 2))
    low = jnp.minimum(one, two)
    high = jnp.maximum(one, two)

    def body(t, _):
        p = t // (2 * chunks)
        u = lax.rem(t, 2 * chunks)
        lone = (p == 0) & ((u == lead) | (u == 10))
        is_first = jnp.where(p == 0, u < chunks + 2, u < chunks) & jnp.logical_not(lone)

        @pl.when(t == 2 * chunks)
        def _():
            prepare(1)
            order_tables()

        @pl.when(is_first)
        def _():
            first_pass(p, jnp.where(p == 0, u - 1 - jnp.where(u > 10, 1, 0), u))

        @pl.when(jnp.logical_not(is_first))
        def _():
            later = u - chunks - 2
            later = later + jnp.where(later >= low, 1, 0)
            later = later + jnp.where(later >= high, 1, 0)
            k = jnp.where(u == lead, one, jnp.where(u == 10, two, later))
            k = jnp.where(p == 0, k, u - chunks)
            lane = lax.rem(k, 4)
            unit = lax.rem(x0 + 1 + lane, 4)
            row = k // 4
            second_pass(p, unit, jnp.where(lax.rem(lane + p, 2) == 0, row, 2 - row))

        @pl.when(t == lead)
        def _():
            sort_decode_rows()
            for d in range(1, ns):
                to_holder(d).start()

        @pl.when(t == 3 * chunks - 1)
        def _():
            decode()

        return 0

    lax.fori_loop(lead, 4 * chunks, body, 0)

    def interleave(p, rank):
        pltpu.make_async_copy(
            gathered.at[pl.ds(0, TP - 1), p, pl.ds(rank * HALF, HALF)],
            gathered.at[pl.ds(0, TP - 1), p, pl.ds(rank * HALF, HALF)],
            recv_sem.at[p, rank],
        ).wait()
        for half in range(2):
            at = pl.multiple_of(rank * HALF + half * 32, 32)
            for b in range(INNER // 256):
                columns = slice(b * 256, (b + 1) * 256)
                stacked = jnp.concatenate(
                    [gathered[g, p, pl.ds(at, 32), columns] for g in range(TP)], axis=0
                )
                first = pl.multiple_of((p * (length // TP) + at) * TP, 256)
                final[pl.ds(first, 256), columns] = dot(perm3[...], stacked).astype(BF16)

    pltpu.make_async_copy(gathered.at[me], gathered.at[me], own_sem).wait()
    lax.fori_loop(0, 3, lambda i, _: (interleave(0, i), 0)[1], 0)

    pltpu.make_async_copy(
        osend.at[pl.ds(0, 16 * (ns - 1))], osend.at[pl.ds(0, 16 * (ns - 1))], osend_sem
    ).wait()
    pltpu.make_async_copy(
        orecv.at[pl.ds(0, 16 * (ns - 1))], orecv.at[pl.ds(0, 16 * (ns - 1))], orecv_sem
    ).wait()
    table = dot_first(perm[...], orecv[...]).astype(BF16)
    for q in range(4):
        for i in range(2):
            part = table[q * n64 + i * n32 : q * n64 + (i + 1) * n32]
            dec_out[:, i, q * 256 : (q + 1) * 256] = part

    turn = 2 - 2 * lax.rem(me, 2)
    lax.fori_loop(0, 3, lambda i, _: (interleave(1, lax.rem(i + turn, 3)), 0)[1], 0)
    for d in range(1, TP):
        peer = lax.rem(me + d, TP)
        pltpu.make_async_copy(gathered.at[peer], gathered.at[peer], send_sem.at[peer]).wait()


def per_device(
    ns,
    prompt_rows,
    prompt_dt,
    decode_rows,
    decode_dt,
    placement,
    conv_weight,
    conv_bias,
    dt_bias,
    a_log,
    skip_gain,
    norm_gain,
):
    length = prompt_rows.shape[1]
    chunks = length // SPAN
    n64, n256 = 4 * ns, 16 * ns
    vmem = pl.BlockSpec(memory_space=pltpu.VMEM)
    hbm = pl.BlockSpec(memory_space=pl.ANY)
    final, dec = pl.pallas_call(
        functools.partial(kernel, ns, length),
        out_shape=(
            pltpu.VMEM((2 * length, INNER), BF16),
            pltpu.VMEM((2 * ns, 2, INNER), BF16),
        ),
        in_specs=[hbm, vmem, vmem, vmem, pl.BlockSpec(memory_space=pltpu.SMEM)] + [vmem] * 6,
        out_specs=(vmem, vmem),
        scratch_shapes=[
            pltpu.VMEM((TP, 2, length // TP, INNER), BF16),
            pltpu.VMEM((2, length, ROW), BF16),
            pltpu.VMEM((2, 16, XBC), BF16),
            pltpu.VMEM((length, INNER), F32),
            pltpu.VMEM((chunks, 4 * SPAN, INNER), BF16),
            pltpu.VMEM((chunks, SPAN, 2 * STATE), F32),
            pltpu.VMEM((chunks, 2 * HEADS, SPAN), BF16),
            pltpu.VMEM((chunks, 2 * HEADS, SPAN), BF16),
            pltpu.VMEM((chunks, 8, INNER), F32),
            pltpu.VMEM((2 * HEADS, INNER), BF16),
            pltpu.VMEM((SPAN, INNER), F32),
            pltpu.VMEM((SPAN, INNER), F32),
            pltpu.VMEM((2, STATE, INNER), F32),
            pltpu.VMEM((8, XBC), F32),
            pltpu.VMEM((1, INNER), F32),
            pltpu.VMEM((n256, n256), BF16),
            pltpu.VMEM((n256, n256), BF16),
            pltpu.VMEM((256, 256), BF16),
            pltpu.VMEM((n256, 640), BF16),
            pltpu.VMEM((n256, 640), BF16),
            pltpu.VMEM((n256, 640), BF16),
            pltpu.VMEM((n256, 640), F32),
            pltpu.VMEM((n256, 256), BF16),
            pltpu.VMEM((n256, 256), BF16),
            pltpu.SemaphoreType.DMA((2, chunks)),
            pltpu.SemaphoreType.DMA((TP,)),
            pltpu.SemaphoreType.DMA((2, 3)),
            pltpu.SemaphoreType.DMA,
            pltpu.SemaphoreType.DMA,
            pltpu.SemaphoreType.DMA,
            pltpu.SemaphoreType.DMA,
            pltpu.SemaphoreType.DMA,
        ],
        compiler_params=pltpu.CompilerParams(
            collective_id=0, has_side_effects=True, vmem_limit_bytes=52 * 2**20
        ),
    )(
        prompt_rows[:, :, 0, :],
        prompt_dt[:, :, 0, :].transpose(0, 2, 1),
        decode_rows[:, 0, :, 0, :],
        decode_dt[:, 0, :, 0, :].transpose(1, 2, 0),
        placement,
        conv_weight[0],
        conv_bias,
        dt_bias,
        a_log,
        skip_gain,
        norm_gain,
    )
    prefill_out = final.reshape(2, length // TP, TP, INNER)
    return prefill_out, dec.reshape(2 * ns, 1, 2, 1, INNER)


def solution(mesh):
    in_specs = (
        P("samp", None, "tp", None),
        P("samp", None, "tp", None),
        P(None, "samp", None, "tp", None),
        P(None, "samp", None, "tp", None),
        P(),
        P("tp", None, None),
        P("tp", None),
        P("tp", None),
        P("tp", None),
        P("tp", None),
        P("tp", None),
    )
    out_specs = (P("samp", "tp", None, None), P(None, "samp", None, "tp", None))
    return jax.shard_map(
        functools.partial(per_device, mesh.shape["samp"]),
        mesh=mesh,
        in_specs=in_specs,
        out_specs=out_specs,
        check_vma=False,
    )
```
